32 devices in a mesh: ctx: 4 (over z), ep: 8 (over y, x, core).
Axes of the slice: x: 2, y: 2, z: 4, core: 2. Of those that a mesh axis runs over, the one named last changes fastest.
Arguments:
- query_act: bfloat16 [512, 2048], P('ctx', 'ep'), may hold values from -6 to 6
- key_act: bfloat16 [512, 2048], P('ctx', 'ep'), may hold values from -6 to 6
- value_act: bfloat16 [512, 2048], P('ctx', 'ep'), may hold values from -6 to 6
- state_init: float32 [16, 128, 128], P('ep'), may hold values from -128 to 128
- head_gain: float32 [2048], P('ep'), may hold values from 0.25 to 1.75
- out_weight: bfloat16 [2048, 3072], P('ctx', 'ep'), may hold values from -0.125 to 0.125
- stream_in: bfloat16 [512, 3072], P('ctx', 'ep'), may hold values from -150 to 150
- model_gain: float32 [3072], replicated, may hold values from 0.25 to 1.75
- expert_ids: int32 [512, 2], P('ctx'), may hold values from 0 to 3, as said below
- expert_slots: int32 [512, 2], P('ctx'), may hold values from 0 to 79, as said below
- route_gates: float32 [512, 2], P('ctx'), may hold values from 0.2 to 1
- gate_weight: bfloat16 [8, 3072, 3072], P('ep', 'ctx'), may hold values from -0.109375 to 0.109375
- up_weight: bfloat16 [8, 3072, 3072], P('ep', 'ctx'), may hold values from -0.109375 to 0.109375
- down_weight: bfloat16 [8, 3072, 3072], P('ep', 'ctx'), may hold values from -0.078125 to 0.078125
- out_grad: bfloat16 [512, 3072], P('ctx', 'ep'), may hold values from -6 to 6
Outputs:
- layer_out: bfloat16 [512, 3072], P('ctx', 'ep')
- grad_query: bfloat16 [512, 2048], P('ctx', 'ep')
- grad_key: bfloat16 [512, 2048], P('ctx', 'ep')
- grad_value: bfloat16 [512, 2048], P('ctx', 'ep')
- grad_state: float32 [16, 128, 128], P('ep')
- grad_stream: bfloat16 [512, 3072], P('ctx', 'ep')
The draws below stay inside these ranges and needn't reach their ends.
Inputs may be any that keep to these rules, and one draw needn't show every extreme that they name: `expert_ids`: within each block of 128 tokens a token's two experts differ; the tokens naming expert e hold the slots 0 to n - 1 of e once each, n being their number; no expert is named by more than 80 tokens of a block, and in every block some expert by exactly 80. `expert_slots`: see expert_ids.
All inputs are finite; a program needn't handle non-finite values.
Results may differ from the reference program's by a relative error of at most 0.02.
Values may be sent and summed in bfloat16 or wider, within the bound.
A program may use at most 64 MiB of HBM per device.

```python
import math
import jax
import jax.numpy as jnp
from jax import lax

D = 3072
HD = 128
EXPERT_FF = 6144
TOK_CTX = 128
HEADS = 16
EXPERTS = 4
TOKENS = 512
C_CH = 80
SLOTS = 320
HBLOCK = 768


def route_tables(key):
    base = jax.random.fold_in(key, 17)
    blocks = TOKENS // TOK_CTX
    tokens_here = TOK_CTX
    remaining = 2 * tokens_here - C_CH
    others = EXPERTS - 1
    common = remaining // others
    extra = remaining % others
    spread = max(1, min(common, C_CH - common - 1))

    def one_block(block_key):
        key_order, key_shift, key_perm, key_swap = jax.random.split(block_key, 4)
        order = jax.random.permutation(key_order, EXPERTS)
        shifts = jax.random.randint(key_shift, (others,), 0, spread)
        moved = shifts - jnp.roll(shifts, -1)
        ranked = jnp.concatenate([jnp.full((1,), C_CH, jnp.int32), (common + (jnp.arange(others) < extra) + moved).astype(jnp.int32)])
        counts = jnp.zeros((EXPERTS,), jnp.int32).at[order].set(ranked)
        ends = jnp.cumsum(counts)
        starts = ends - counts
        places = jnp.arange(2 * tokens_here, dtype=jnp.int32)
        labels = jnp.sum((ends[None, :] <= places[:, None]).astype(jnp.int32), 1)
        owned = labels[:, None] == jnp.arange(EXPERTS)[None, :]
        slot_of = places - jnp.sum(jnp.where(owned, starts[None, :], 0), 1)
        pair_ids = jnp.stack([labels[:tokens_here], labels[tokens_here:]], -1)
        pair_slots = jnp.stack([slot_of[:tokens_here], slot_of[tokens_here:]], -1)
        shuffle = jax.random.permutation(key_perm, tokens_here)
        pair_ids = pair_ids[shuffle]
        pair_slots = pair_slots[shuffle]
        flips = jax.random.randint(key_swap, (tokens_here, 1), 0, 2) == 1
        pair_ids = jnp.where(flips, pair_ids[:, ::-1], pair_ids)
        pair_slots = jnp.where(flips, pair_slots[:, ::-1], pair_slots)
        return (pair_ids.astype(jnp.int32), pair_slots.astype(jnp.int32))
    block_keys = jax.vmap(lambda index: jax.random.fold_in(base, index))(jnp.arange(blocks))
    all_ids, all_slots = jax.vmap(one_block)(block_keys)
    return (all_ids.reshape(TOKENS, 2), all_slots.reshape(TOKENS, 2))


def draw_expert_ids(key, part):
    return route_tables(key)[0]


def draw_expert_slots(key, part):
    return route_tables(key)[1]


def draw_stream_in(key, part):
    key_cols, key_rows, key_vals = jax.random.split(key, 3)
    rising = 1.0 + 2.0 * jnp.arange(D, dtype=jnp.float32)[None, :] / D
    column_scale = jnp.exp(jax.random.uniform(key_cols, (1, D)) * math.log(10.0)) * rising
    row_scale = jnp.exp(jax.random.uniform(key_rows, (TOKENS, 1)) * math.log(4.0))
    values = jnp.clip(jax.random.normal(key_vals, (TOKENS, D)), -6.0, 6.0)
    return (0.12 * values * row_scale * column_scale).astype(jnp.bfloat16)


def level_of(rng, dims, cuts, smallest, high):
    def one(axis_at, parts):
        draws = jax.random.uniform(jax.random.fold_in(jax.random.fold_in(rng, 6), axis_at), (parts,), jnp.float32, smallest / len(cuts), high / len(cuts))
        return jnp.repeat(jnp.exp(draws), dims[axis_at] // parts).reshape((-1,) + (1,) * (len(dims) - axis_at - 1))

    level = one(*cuts[0])
    for cut in cuts[1:]:
        level = level * one(*cut)
    return level


def normal_values(key, dims, width, bound, shards=(), kind=jnp.bfloat16):
    result = width * jax.random.normal(key, dims, jnp.float32)
    if shards:
        result = result * level_of(key, dims, shards, -0.22, 0.18)
    return jnp.clip(result, -bound, bound).astype(kind)


def setup_inputs(seed: int = 0) -> dict:
    key_list = jax.random.split(jax.random.key(seed), 16)
    query_act = normal_values(key_list[0], (TOKENS, HEADS * HD), 1.0, 6.0, ((0, 4), (1, 8)))
    key_act = normal_values(key_list[1], (TOKENS, HEADS * HD), 1.0, 6.0, ((0, 4), (1, 8)))
    value_act = normal_values(key_list[2], (TOKENS, HEADS * HD), 1.0, 6.0, ((0, 4), (1, 8)))
    state_init = normal_values(key_list[3], (HEADS, HD, HD), 20.0, 128.0, ((0, 8),), jnp.float32)
    head_gain = jnp.clip(1.0 + 0.15 * jax.random.normal(key_list[4], (HEADS * HD,), jnp.float32), 0.25, 1.75)
    out_weight = normal_values(key_list[5], (HEADS * HD, D), (HEADS * HD) ** -0.5, 0.125, ((0, 4), (1, 8)))
    stream_in = draw_stream_in(jax.random.fold_in(key_list[15], 71), 0)
    model_gain = jnp.clip(1.0 + 0.15 * jax.random.normal(key_list[7], (D,), jnp.float32), 0.25, 1.75)
    expert_ids = draw_expert_ids(jax.random.fold_in(key_list[15], 71), 0)
    expert_slots = draw_expert_slots(jax.random.fold_in(key_list[15], 71), 0)
    route_gates = jnp.clip(0.2 + 0.8 * jax.random.uniform(key_list[10], (TOKENS, 2), jnp.float32) ** level_of(key_list[10], (TOKENS, 2), ((0, 4),), -0.2, 0.2), 0.2, 1.0)
    gate_weight = normal_values(key_list[11], (2 * EXPERTS, EXPERT_FF // 2, D), D ** -0.5, 0.109375, ((0, 8), (1, 4)))
    up_weight = normal_values(key_list[12], (2 * EXPERTS, EXPERT_FF // 2, D), D ** -0.5, 0.109375, ((0, 8), (1, 4)))
    down_weight = normal_values(key_list[13], (2 * EXPERTS, EXPERT_FF // 2, D), EXPERT_FF ** -0.5, 0.078125, ((0, 8), (1, 4)))
    out_grad = normal_values(key_list[14], (TOKENS, D), 1.0, 6.0, ((0, 4), (1, 8)))
    return {"query_act": query_act, "key_act": key_act, "value_act": value_act, "state_init": state_init, "head_gain": head_gain, "out_weight": out_weight, "stream_in": stream_in, "model_gain": model_gain, "expert_ids": expert_ids, "expert_slots": expert_slots, "route_gates": route_gates, "gate_weight": gate_weight, "up_weight": up_weight, "down_weight": down_weight, "out_grad": out_grad}


def head_normalize(attended, gain):
    factor = lax.rsqrt(lax.optimization_barrier(jnp.mean(attended * attended, -1, keepdims=True)) + 1e-06)
    return attended * factor * gain

def model_normalize(stream_f, model_gain):
    factor = lax.rsqrt(lax.optimization_barrier(jnp.mean(stream_f * stream_f, -1, keepdims=True)) + 1e-05)
    return stream_f * factor * model_gain

def round_bf(value):
    return lax.optimization_barrier(value.astype(jnp.bfloat16)).astype(jnp.float32)

def reference(query_act, key_act, value_act, state_init, head_gain, out_weight, stream_in, model_gain, expert_ids, expert_slots, route_gates, gate_weight, up_weight, down_weight, out_grad):
    f32 = jnp.float32
    high = lax.Precision.HIGHEST
    blocks = TOKENS // TOK_CTX
    query4 = query_act.astype(f32).reshape(blocks, TOK_CTX, HEADS, HD)
    key4 = key_act.astype(f32).reshape(blocks, TOK_CTX, HEADS, HD)
    value4 = value_act.astype(f32).reshape(blocks, TOK_CTX, HEADS, HD)
    kv_blocks = jnp.einsum('cthd,cthe->chde', key4, value4)
    running = jnp.cumsum(kv_blocks, 0)
    before = jnp.concatenate([jnp.zeros_like(kv_blocks[:1]), running[:-1]], 0)
    prefix = state_init[None] + before
    causal = jnp.arange(TOK_CTX)[:, None] >= jnp.arange(TOK_CTX)[None, :]
    scores = jnp.einsum('cthd,cshd->chts', query4, key4)
    scores_bf = jnp.where(causal[None, None], scores, 0.0).astype(jnp.bfloat16)
    inside = jnp.einsum('chts,cshe->cthe', scores_bf.astype(f32), value4)
    from_state = jnp.einsum('cthd,chde->cthe', query4, prefix, precision=high)
    attended = from_state + inside
    gain_heads = head_gain.reshape(HEADS, HD)
    normed_heads = head_normalize(attended, gain_heads).astype(jnp.bfloat16).reshape(TOKENS, HEADS * HD)
    stream = (stream_in.astype(f32) + jnp.dot(normed_heads, out_weight, preferred_element_type=f32)).astype(jnp.bfloat16)
    stream_f = stream.astype(f32)
    model_in = model_normalize(stream_f, model_gain).astype(jnp.bfloat16)
    block_of = (jnp.arange(TOKENS) // TOK_CTX).astype(jnp.int32)
    slot_row = block_of[:, None] * C_CH + expert_slots
    spread_in = jnp.broadcast_to(model_in[:, None, :], (TOKENS, 2, D))
    slot_in = jnp.zeros((EXPERTS, SLOTS, D), jnp.bfloat16).at[expert_ids, slot_row].set(spread_in)
    half_units = EXPERT_FF // 2
    saved = []
    outputs = []
    for expert in range(EXPERTS):
        w_gate = jnp.concatenate([gate_weight[expert], gate_weight[expert + EXPERTS]], 0).T
        w_up = jnp.concatenate([up_weight[expert], up_weight[expert + EXPERTS]], 0).T
        w_down = jnp.concatenate([down_weight[expert], down_weight[expert + EXPERTS]], 0)
        pre_gate = jnp.dot(slot_in[expert], w_gate, preferred_element_type=f32)
        pre_up = jnp.dot(slot_in[expert], w_up, preferred_element_type=f32)
        activated = (jax.nn.silu(pre_gate) * pre_up).astype(jnp.bfloat16)
        halves = []
        for half in range(2):
            summed = jnp.zeros((SLOTS, D), f32)
            for index in range(half_units // HBLOCK):
                lower = half * half_units + index * HBLOCK
                term = jnp.dot(activated[:, lower:lower + HBLOCK], w_down[lower:lower + HBLOCK], preferred_element_type=f32)
                summed = summed + round_bf(term)
            halves.append(summed.astype(jnp.bfloat16).astype(f32))
        outputs.append(halves[0] + halves[1])
        saved.append((w_gate, w_up, w_down, pre_gate, pre_up))
    expert_out = jnp.stack(outputs, 0)
    expert_mix = lax.optimization_barrier(jnp.sum(route_gates[:, :, None] * expert_out[expert_ids, slot_row], 1))
    layer_out = (stream_f + expert_mix).astype(jnp.bfloat16)
    grad_out = out_grad.astype(f32)
    gated = (route_gates[:, :, None] * grad_out[:, None, :]).astype(jnp.bfloat16)
    grad_rows = jnp.zeros((EXPERTS, SLOTS, D), jnp.bfloat16).at[expert_ids, slot_row].set(gated)
    back = []
    for expert in range(EXPERTS):
        w_gate, w_up, w_down, pre_gate, pre_up = saved[expert]
        grad_act = jnp.dot(grad_rows[expert], w_down.T, preferred_element_type=f32)
        gate_sig = jax.nn.sigmoid(pre_gate)
        grad_gate_pre = (grad_act * pre_up * gate_sig * (1.0 + pre_gate * (1.0 - gate_sig))).astype(jnp.bfloat16)
        grad_up_pre = (grad_act * pre_gate * gate_sig).astype(jnp.bfloat16)
        halves = []
        for half in range(2):
            summed = jnp.zeros((SLOTS, D), f32)
            for index in range(half_units // HBLOCK):
                lower = half * half_units + index * HBLOCK
                term = jnp.dot(grad_gate_pre[:, lower:lower + HBLOCK], w_gate[:, lower:lower + HBLOCK].T, preferred_element_type=f32)
                term = term + jnp.dot(grad_up_pre[:, lower:lower + HBLOCK], w_up[:, lower:lower + HBLOCK].T, preferred_element_type=f32)
                summed = summed + round_bf(term)
            halves.append(summed.astype(jnp.bfloat16).astype(f32))
        back.append(halves[0] + halves[1])
    grad_slots_all = jnp.stack(back, 0)
    grad_model_in = lax.optimization_barrier(jnp.sum(grad_slots_all[expert_ids, slot_row], 1))
    norm_pull = jax.vjp(lambda value: model_normalize(value, model_gain), stream_f)[1]
    grad_stream = (grad_out + norm_pull(grad_model_in)[0]).astype(jnp.bfloat16)
    grad_heads = jnp.dot(grad_stream, out_weight.T, preferred_element_type=f32).reshape(blocks, TOK_CTX, HEADS, HD)
    head_pull = jax.vjp(lambda value: head_normalize(value, gain_heads), attended)[1]
    grad_attended = head_pull(grad_heads)[0].astype(jnp.bfloat16).astype(f32)
    state_part = jnp.einsum('cthd,cthe->chde', query4, grad_attended)
    reverse_run = jnp.cumsum(state_part[::-1], 0)[::-1]
    later = jnp.concatenate([reverse_run[1:], jnp.zeros_like(state_part[:1])], 0)
    grad_state = lax.optimization_barrier(jnp.sum(state_part, 0))
    grad_scores = jnp.einsum('cthe,cshe->chts', grad_attended, value4)
    grad_masked = jnp.where(causal[None, None], grad_scores, 0.0).astype(jnp.bfloat16).astype(f32)
    grad_query = jnp.einsum('cthe,chde->cthd', grad_attended, prefix, precision=high) + jnp.einsum('chts,cshd->cthd', grad_masked, key4)
    grad_key = jnp.einsum('cthe,chde->cthd', value4, later, precision=high) + jnp.einsum('chts,cthd->cshd', grad_masked, query4)
    grad_value = jnp.einsum('cthd,chde->cthe', key4, later, precision=high) + jnp.einsum('chts,cthe->cshe', scores_bf.astype(f32), grad_attended)
    shape_out = (TOKENS, HEADS * HD)
    return (layer_out, grad_query.astype(jnp.bfloat16).reshape(shape_out), grad_key.astype(jnp.bfloat16).reshape(shape_out), grad_value.astype(jnp.bfloat16).reshape(shape_out), grad_state, grad_stream)
```

```python
import functools

import jax
import jax.numpy as jnp
from jax import lax
from jax.experimental import pallas as pl
from jax.experimental.pallas import tpu as pltpu
from jax.sharding import PartitionSpec as P

MESH = pl.DeviceIdType.MESH


def exchange_kernel(axis, sources, places, *refs):
    count = len(sources)
    inputs, outputs = refs[:count], refs[count : 2 * count]
    send_sem, recv_sem, own_sem = refs[2 * count :]
    total = lax.axis_size(axis)
    me = lax.axis_index(axis)
    barrier = pltpu.get_barrier_semaphore()
    for step in range(1, total):
        pl.semaphore_signal(
            barrier, inc=1, device_id={axis: lax.rem(me + step, total)}, device_id_type=MESH
        )
    pl.semaphore_wait(barrier, total - 1)
    copies = []
    for step in range(1, total):
        peer = lax.rem(me + step, total)
        for item in range(count):
            copy = pltpu.make_async_remote_copy(
                src_ref=sources[item](inputs[item], peer),
                dst_ref=places[item](outputs[item], me),
                send_sem=send_sem.at[item, step - 1],
                recv_sem=recv_sem.at[item, step - 1],
                device_id={axis: peer},
                device_id_type=MESH,
            )
            copy.start()
            copies.append(copy)
    for item in range(count):
        own = pltpu.make_async_copy(
            sources[item](inputs[item], me), places[item](outputs[item], me), own_sem.at[item]
        )
        own.start()
        copies.append(own)
    for copy in copies:
        copy.wait()


def whole_ref(ref, peer):
    return ref


def leading(ref, place):
    return ref.at[place]


def second(ref, place):
    return ref.at[:, place]


def lanes(width):
    def pick(ref, place):
        start = pl.multiple_of(place * width, width)
        if len(ref.shape) == 2:
            return ref.at[:, pl.ds(start, width)]
        return ref.at[:, :, pl.ds(start, width)]

    return pick


def exchange(axis, ident, items):
    total = lax.axis_size(axis)
    count = len(items)
    result = pl.pallas_call(
        functools.partial(
            exchange_kernel, axis, [item[1] for item in items], [item[3] for item in items]
        ),
        out_shape=[jax.ShapeDtypeStruct(item[2], item[0].dtype) for item in items],
        in_specs=[pl.BlockSpec(memory_space=pl.ANY)] * count,
        out_specs=[pl.BlockSpec(memory_space=pl.ANY)] * count,
        scratch_shapes=[
            pltpu.SemaphoreType.DMA((count, total - 1)),
            pltpu.SemaphoreType.DMA((count, total - 1)),
            pltpu.SemaphoreType.DMA((count,)),
        ],
        compiler_params=pltpu.CompilerParams(collective_id=ident, has_side_effects=True),
        name=f"exchange_{ident}",
    )(*[item[0] for item in items])
    return result


def column_parts(value, parts):
    width = value.shape[-1] // parts
    if width % 128 == 0:
        return value, lanes(width)
    split = value.reshape(value.shape[:-1] + (parts, width))
    return jnp.moveaxis(split, -2, 0), leading


def spread_kernel(block_ref, all_ref, z_send, z_recv, xy_send, xy_recv, pair_send, pair_recv, own_sem):
    rows, width = block_ref.shape
    blocks = lax.axis_size("ctx")
    chips = lax.axis_size("ep") // 2
    my_block = lax.axis_index("ctx")
    my_ep = lax.axis_index("ep")
    chip = my_ep // 2
    core = lax.rem(my_ep, 2)

    def at(block, place):
        row = pl.multiple_of(block * rows, rows)
        column = pl.multiple_of(place * width, width)
        return all_ref.at[pl.ds(row, rows), pl.ds(column, width)]

    barrier = pltpu.get_barrier_semaphore()
    for step in range(1, blocks):
        pl.semaphore_signal(
            barrier, inc=1, device_id={"ctx": lax.rem(my_block + step, blocks)}, device_id_type=MESH
        )
    for step in range(1, chips):
        pl.semaphore_signal(
            barrier,
            inc=1,
            device_id={"ep": 2 * lax.rem(chip + step, chips) + core},
            device_id_type=MESH,
        )
    pl.semaphore_signal(
        barrier, inc=1, device_id={"ep": 2 * chip + 1 - core}, device_id_type=MESH
    )
    pl.semaphore_wait(barrier, blocks + chips - 1)
    z_copies = []
    for step in range(1, blocks):
        copy = pltpu.make_async_remote_copy(
            src_ref=block_ref,
            dst_ref=at(my_block, my_ep),
            send_sem=z_send.at[step - 1],
            recv_sem=z_recv.at[step - 1],
            device_id={"ctx": lax.rem(my_block + step, blocks)},
            device_id_type=MESH,
        )
        copy.start()
        z_copies.append(copy)
    own = pltpu.make_async_copy(block_ref, at(my_block, my_ep), own_sem)
    own.start()
    xy_copies = {}
    pair_copies = []

    def to_pair(back, turn):
        block = lax.rem(my_block - back + blocks, blocks)
        place = 2 * lax.rem(chip - turn + chips, chips) + core
        source = block_ref if back == 0 and turn == 0 else at(block, place)
        copy = pltpu.make_async_remote_copy(
            src_ref=source,
            dst_ref=at(block, place),
            send_sem=pair_send.at[back * chips + turn],
            recv_sem=pair_recv.at[back * chips + turn],
            device_id={"ep": 2 * chip + 1 - core},
            device_id_type=MESH,
        )
        copy.start()
        pair_copies.append(copy)

    for back in range(blocks + 1):
        if back < blocks:
            block = lax.rem(my_block - back + blocks, blocks)
            if back > 0:
                z_copies[back - 1].wait_recv()
            for step in range(1, chips):
                slot = back * (chips - 1) + step - 1
                copy = pltpu.make_async_remote_copy(
                    src_ref=block_ref if back == 0 else at(block, my_ep),
                    dst_ref=at(block, my_ep),
                    send_sem=xy_send.at[slot],
                    recv_sem=xy_recv.at[slot],
                    device_id={"ep": 2 * lax.rem(chip + step, chips) + core},
                    device_id_type=MESH,
                )
                copy.start()
                xy_copies[back, step] = copy
            to_pair(back, 0)
        if back > 0:
            for step in range(1, chips):
                xy_copies[back - 1, step].wait_recv()
                to_pair(back - 1, step)
    own.wait()
    for copy in z_copies + list(xy_copies.values()):
        copy.wait_send()
    for copy in pair_copies:
        copy.wait()


def spread(block, ident):
    blocks = lax.axis_size("ctx")
    parts = lax.axis_size("ep")
    rows, width = block.shape
    if blocks * parts > 64 or width % 128:
        return lax.all_gather(
            lax.all_gather(block, "ep", axis=1, tiled=True), "ctx", axis=0, tiled=True
        )
    chips = parts // 2
    dma = pltpu.SemaphoreType.DMA
    return pl.pallas_call(
        spread_kernel,
        out_shape=jax.ShapeDtypeStruct((blocks * rows, parts * width), block.dtype),
        in_specs=[pl.BlockSpec(memory_space=pl.ANY)],
        out_specs=pl.BlockSpec(memory_space=pl.ANY),
        scratch_shapes=[
            dma((blocks - 1,)),
            dma((blocks - 1,)),
            dma((blocks * (chips - 1),)),
            dma((blocks * (chips - 1),)),
            dma((blocks * chips,)),
            dma((blocks * chips,)),
            dma,
        ],
        compiler_params=pltpu.CompilerParams(collective_id=ident, has_side_effects=True),
        name=f"spread_{ident}",
    )(block)

def head_normalize(attended, gain):
    factor = lax.rsqrt(jnp.mean(attended * attended, -1, keepdims=True) + 1e-06)
    return attended * factor * gain


def contract_last(left, right):
    return lax.dot_general(
        left, right, (((1,), (1,)), ((), ())), preferred_element_type=jnp.float32
    )


def local(
    query_act,
    key_act,
    value_act,
    state_init,
    head_gain,
    out_weight,
    stream_in,
    model_gain,
    expert_ids,
    expert_slots,
    route_gates,
    gate_weight,
    up_weight,
    down_weight,
    out_grad,
):
    f32 = jnp.float32
    bf16 = jnp.bfloat16
    high = lax.Precision.HIGHEST
    ep_count = lax.axis_size("ep")
    ctx_count = lax.axis_size("ctx")
    expert_count = ep_count // 2
    my_ep = lax.axis_index("ep")
    my_ctx = lax.axis_index("ctx")
    tokens_here = query_act.shape[0]
    head_count = state_init.shape[0]
    head_size = state_init.shape[1]
    heads_width = head_count * head_size
    model_width = model_gain.shape[0]
    columns = stream_in.shape[1]
    capacity = 5 * tokens_here // (2 * expert_count)
    slots_all = ctx_count * capacity
    w_cols = lax.all_gather(out_weight, "ctx", axis=0, tiled=True)
    grads_all = lax.all_gather(
        lax.all_gather(out_grad, "ctx", axis=0, tiled=True), "ep", axis=1, tiled=True
    )
    query3 = query_act.reshape(tokens_here, head_count, head_size)
    key3 = key_act.reshape(tokens_here, head_count, head_size)
    value3 = value_act.reshape(tokens_here, head_count, head_size)
    kv_own = jnp.einsum("thd,the->hde", key3, value3, preferred_element_type=f32)
    meta = jnp.concatenate(
        [expert_ids.T.astype(f32), expert_slots.T.astype(f32), route_gates.T, route_gates.T], 0
    )
    kv_all, meta_all = exchange(
        "ctx",
        1,
        [
            (kv_own.astype(bf16), whole_ref, (ctx_count,) + kv_own.shape, leading),
            (meta, whole_ref, (ctx_count,) + meta.shape, leading),
        ],
    )
    earlier = (jnp.arange(ctx_count) < my_ctx).astype(f32)
    prefix = state_init + jnp.sum(earlier[:, None, None, None] * kv_all.astype(f32), 0)
    causal = jnp.arange(tokens_here)[:, None] >= jnp.arange(tokens_here)[None, :]
    scores = jnp.einsum("thd,shd->hts", query3, key3, preferred_element_type=f32)
    scores_bf = jnp.where(causal[None], scores, 0.0).astype(bf16)
    inside = jnp.einsum("hts,she->the", scores_bf, value3, preferred_element_type=f32)
    from_state = jnp.einsum("thd,hde->the", query3.astype(f32), prefix, precision=high)
    attended = from_state + inside
    gain_heads = head_gain.reshape(head_count, head_size)
    normed_heads = (
        head_normalize(attended, gain_heads).astype(bf16).reshape(tokens_here, heads_width)
    )
    normed_all = exchange(
        "ep",
        2,
        [(normed_heads, whole_ref, (tokens_here, ep_count * heads_width), lanes(heads_width))],
    )[0]
    attn_proj = jnp.dot(normed_all, w_cols, preferred_element_type=f32)
    stream = (stream_in.astype(f32) + attn_proj).astype(bf16)
    stream_f = stream.astype(f32)
    gain_cols = lax.dynamic_slice_in_dim(model_gain, my_ep * columns, columns, 0)
    all_rows = spread(stream, 3).astype(f32)
    scale_all = lax.rsqrt(jnp.mean(all_rows * all_rows, -1, keepdims=True) + 1e-05)
    model_in = (all_rows * scale_all * model_gain).astype(bf16)
    row_scale = lax.dynamic_slice_in_dim(scale_all, my_ctx * tokens_here, tokens_here, 0)
    ids_all = meta_all[:, 0:2]
    slots_of = meta_all[:, 2:4]
    gates_all = meta_all[:, 4:6]
    slot_iota = jnp.arange(capacity).astype(f32)
    my_expert = lax.rem(my_ep, expert_count).astype(f32)
    own_hits = (ids_all[:, :, None, :] == my_expert) & (
        slots_of[:, :, None, :] == slot_iota[None, None, :, None]
    )
    own_select = jnp.sum(own_hits.astype(f32), 1).astype(bf16)
    slot_gates = jnp.sum(jnp.where(own_hits, gates_all[:, :, None, :], 0.0), (1, 3))

    def pick_rows(rows):
        return jnp.einsum(
            "cst,ctd->csd",
            own_select,
            rows.reshape(ctx_count, tokens_here, model_width),
            preferred_element_type=f32,
        )

    grad_rows = (
        (pick_rows(grads_all) * slot_gates[:, :, None])
        .astype(bf16)
        .reshape(slots_all, model_width)
    )
    w_gate = gate_weight[0]
    w_up = up_weight[0]
    w_down = down_weight[0]
    portion = pick_rows(model_in).astype(bf16).reshape(slots_all, model_width)
    pre_gate = contract_last(portion, w_gate)
    pre_up = contract_last(portion, w_up)
    gate_sig = jax.nn.sigmoid(pre_gate)
    activated = (pre_gate * gate_sig * pre_up).astype(bf16)
    half_out = lax.psum_scatter(
        jnp.dot(activated, w_down, preferred_element_type=f32).astype(bf16),
        "ctx",
        scatter_dimension=0,
        tiled=True,
    )
    grad_act = contract_last(grad_rows, w_down)
    grad_gate_pre = (grad_act * pre_up * gate_sig * (1.0 + pre_gate * (1.0 - gate_sig))).astype(
        bf16
    )
    grad_up_pre = (grad_act * pre_gate * gate_sig).astype(bf16)
    grad_half = (
        jnp.dot(grad_gate_pre, w_gate, preferred_element_type=f32)
        + jnp.dot(grad_up_pre, w_up, preferred_element_type=f32)
    ).astype(bf16)
    grad_parts, part_of = column_parts(
        grad_half.reshape(ctx_count, capacity, model_width), ep_count
    )
    grad_back = exchange(
        "ep", 4, [(grad_parts, part_of, (ctx_count, ep_count, capacity, columns), second)]
    )[0]
    expert_of = (jnp.arange(ep_count) % expert_count).astype(f32)
    hits = (ids_all[:, :, :, None, None] == expert_of[None, None, None, :, None]) & (
        slots_of[:, :, :, None, None] == slot_iota[None, None, None, None, :]
    )
    picks = jnp.sum(hits.astype(f32), 1).astype(bf16)
    grad_tokens = jnp.einsum(
        "ctr,crd->ctd",
        picks.reshape(ctx_count, tokens_here, ep_count * capacity),
        grad_back.reshape(ctx_count, ep_count * capacity, columns),
        preferred_element_type=f32,
    ).astype(bf16)
    grad_terms = exchange("ctx", 5, [(grad_tokens, leading, grad_tokens.shape, leading)])[0]
    grad_model_in = jnp.sum(grad_terms.astype(f32), 0)
    scaled_grad = grad_model_in * gain_cols
    inner_own = jnp.sum(stream_f * scaled_grad, -1)
    inner_terms = exchange(
        "ep",
        6,
        [
            (
                jnp.broadcast_to(inner_own[None], (8, tokens_here)),
                whole_ref,
                (ep_count, 8, tokens_here),
                leading,
            )
        ],
    )[0]
    inner_sum = jnp.sum(inner_terms[:, 0], 0)
    grad_out = out_grad.astype(f32)
    grad_stream = (
        grad_out
        + row_scale * scaled_grad
        - stream_f * row_scale**3 * inner_sum[:, None] / model_width
    ).astype(bf16)
    head_parts = contract_last(grad_stream, w_cols).astype(bf16)
    out_parts, out_of = column_parts(half_out, ep_count)
    head_terms, returned = exchange(
        "ep",
        7,
        [
            (head_parts, lanes(heads_width), (ep_count, tokens_here, heads_width), leading),
            (out_parts, out_of, (ep_count, capacity, columns), leading),
        ],
    )
    grad_heads = jnp.sum(head_terms.astype(f32), 0)
    local_hits = (expert_ids[:, :, None, None] == (jnp.arange(ep_count) % expert_count)[:, None]) & (
        expert_slots[:, :, None, None] == jnp.arange(capacity)
    )
    dest_weights = jnp.sum(
        local_hits.astype(f32) * route_gates[:, :, None, None], 1
    ).reshape(tokens_here, ep_count * capacity)
    expert_mix = jnp.dot(
        dest_weights, returned.reshape(ep_count * capacity, columns).astype(f32), precision=high
    )
    layer_out = (stream_f + expert_mix).astype(bf16)
    head_pull = jax.vjp(lambda value: head_normalize(value, gain_heads), attended)[1]
    grad_attended = head_pull(grad_heads.reshape(tokens_here, head_count, head_size))[0].astype(
        bf16
    )
    state_part = jnp.einsum("thd,the->hde", query3, grad_attended, preferred_element_type=f32)
    state_all = exchange(
        "ctx", 8, [(state_part.astype(bf16), whole_ref, (ctx_count,) + state_part.shape, leading)]
    )[0].astype(f32)
    after = (jnp.arange(ctx_count) > my_ctx).astype(f32)
    later_sum = jnp.sum(after[:, None, None, None] * state_all, 0)
    state_total = jnp.sum(state_all, 0)
    grad_scores = jnp.einsum("the,she->hts", grad_attended, value3, preferred_element_type=f32)
    grad_masked = jnp.where(causal[None], grad_scores, 0.0).astype(jnp.bfloat16)
    grad_att_f = grad_attended.astype(f32)
    grad_query = jnp.einsum("the,hde->thd", grad_att_f, prefix, precision=high) + jnp.einsum(
        "hts,shd->thd", grad_masked, key3, preferred_element_type=f32
    )
    grad_key = jnp.einsum(
        "the,hde->thd", value3.astype(f32), later_sum, precision=high
    ) + jnp.einsum("hts,thd->shd", grad_masked, query3, preferred_element_type=f32)
    grad_value = jnp.einsum(
        "thd,hde->the", key3.astype(f32), later_sum, precision=high
    ) + jnp.einsum("hts,the->she", scores_bf, grad_attended, preferred_element_type=f32)
    flat_shape = (tokens_here, head_count * head_size)
    return (
        layer_out,
        grad_query.astype(jnp.bfloat16).reshape(flat_shape),
        grad_key.astype(jnp.bfloat16).reshape(flat_shape),
        grad_value.astype(jnp.bfloat16).reshape(flat_shape),
        state_total,
        grad_stream,
    )


def solution(mesh):
    return jax.shard_map(
        local,
        mesh=mesh,
        in_specs=(
            P("ctx", "ep"),
            P("ctx", "ep"),
            P("ctx", "ep"),
            P("ep", None, None),
            P("ep"),
            P("ctx", "ep"),
            P("ctx", "ep"),
            P(),
            P("ctx", None),
            P("ctx", None),
            P("ctx", None),
            P("ep", "ctx", None),
            P("ep", "ctx", None),
            P("ep", "ctx", None),
            P("ctx", "ep"),
        ),
        out_specs=(
            P("ctx", "ep"),
            P("ctx", "ep"),
            P("ctx", "ep"),
            P("ctx", "ep"),
            P("ep", None, None),
            P("ctx", "ep"),
        ),
        check_vma=False,
    )
```

```python
import functools

import jax
import jax.numpy as jnp
from jax import lax
from jax.experimental import pallas as pl
from jax.experimental.pallas import tpu as pltpu
from jax.sharding import PartitionSpec as P

MESH = pl.DeviceIdType.MESH


def greet(axes):
    barrier = pltpu.get_barrier_semaphore()
    expected = 0
    for axis in axes:
        total = lax.axis_size(axis)
        for step in range(1, total):
            pl.semaphore_signal(
                barrier,
                inc=1,
                device_id={axis: lax.rem(lax.axis_index(axis) + step, total)},
                device_id_type=MESH,
            )
        expected += total - 1
    pl.semaphore_wait(barrier, expected)


def exchange_kernel(axes, sources, places, *refs):
    count = len(sources)
    inputs, outputs = refs[:count], refs[count : 2 * count]
    send_sem, recv_sem, own_sem = refs[2 * count :]
    greet(sorted(set(axes)))
    copies = []
    for item in range(count):
        axis = axes[item]
        total = lax.axis_size(axis)
        me = lax.axis_index(axis)
        for step in range(1, total):
            peer = lax.rem(me + step, total)
            copy = pltpu.make_async_remote_copy(
                src_ref=sources[item](inputs[item], peer),
                dst_ref=places[item](outputs[item], me),
                send_sem=send_sem.at[item, step - 1],
                recv_sem=recv_sem.at[item, step - 1],
                device_id={axis: peer},
                device_id_type=MESH,
            )
            copy.start()
            copies.append(copy)
    for item in range(count):
        me = lax.axis_index(axes[item])
        own = pltpu.make_async_copy(
            sources[item](inputs[item], me), places[item](outputs[item], me), own_sem.at[item]
        )
        own.start()
        copies.append(own)
    for copy in copies:
        copy.wait()


def whole_ref(ref, peer):
    return ref


def leading(ref, place):
    return ref.at[place]


def second(ref, place):
    return ref.at[:, place]


def lanes(width):
    def pick(ref, place):
        start = pl.multiple_of(place * width, width)
        if len(ref.shape) == 2:
            return ref.at[:, pl.ds(start, width)]
        return ref.at[:, :, pl.ds(start, width)]

    return pick


def exchange(axis, ident, items):
    axes = [item[4] if len(item) > 4 else axis for item in items]
    total = max(lax.axis_size(name) for name in axes)
    count = len(items)
    result = pl.pallas_call(
        functools.partial(
            exchange_kernel, axes, [item[1] for item in items], [item[3] for item in items]
        ),
        out_shape=[jax.ShapeDtypeStruct(item[2], item[0].dtype) for item in items],
        in_specs=[pl.BlockSpec(memory_space=pl.ANY)] * count,
        out_specs=[pl.BlockSpec(memory_space=pl.ANY)] * count,
        scratch_shapes=[
            pltpu.SemaphoreType.DMA((count, total - 1)),
            pltpu.SemaphoreType.DMA((count, total - 1)),
            pltpu.SemaphoreType.DMA((count,)),
        ],
        compiler_params=pltpu.CompilerParams(collective_id=ident, has_side_effects=True),
        name=f"exchange_{ident}",
    )(*[item[0] for item in items])
    return result


def column_parts(value, parts):
    width = value.shape[-1] // parts
    if width % 128 == 0:
        return value, lanes(width)
    split = value.reshape(value.shape[:-1] + (parts, width))
    return jnp.moveaxis(split, -2, 0), leading


def combine_kernel(
    rows_ref, picks_ref, stream_ref, gain_ref, grad_ref, inner_ref,
    landed, outgoing, arrived, inner_own, inner_all,
    own_sem, send_sem, recv_sem, z_send, z_recv, i_send, i_recv,
):
    f32 = jnp.float32
    blocks = lax.axis_size("ctx")
    parts = lax.axis_size("ep")
    experts = picks_ref.shape[1]
    width = stream_ref.shape[1]
    my_block = lax.axis_index("ctx")
    my_ep = lax.axis_index("ep")
    greet(["ctx", "ep"])

    def block_at(step):
        return lax.rem(my_block + step, blocks)

    def columns_of(place):
        return pl.ds(pl.multiple_of(place * width, width), width)

    order = list(range(1, blocks)) + [0]
    copies = {}
    for step in order:
        block = block_at(step)
        for turn in range(1, parts):
            peer = lax.rem(my_ep + turn, parts)
            copy = pltpu.make_async_remote_copy(
                src_ref=rows_ref.at[block, :, columns_of(peer)],
                dst_ref=landed.at[block, my_ep],
                send_sem=send_sem.at[step, turn - 1],
                recv_sem=recv_sem.at[step, turn - 1],
                device_id={"ep": peer},
                device_id_type=MESH,
            )
            copy.start()
            copies[step, turn] = copy
    own = pltpu.make_async_copy(
        rows_ref.at[:, :, columns_of(my_ep)], landed.at[:, my_ep], own_sem
    )
    own.start()
    own.wait()
    z_copies = []
    total = None
    for step in order:
        block = block_at(step)
        for turn in range(1, parts):
            copies[step, turn].wait_recv()
        total = jnp.dot(picks_ref[block, 0], landed[block, 0], preferred_element_type=f32)
        for place in range(1, parts):
            total += jnp.dot(
                picks_ref[block, place % experts],
                landed[block, place],
                preferred_element_type=f32,
            )
        if step:
            outgoing[step - 1] = total.astype(outgoing.dtype)
            copy = pltpu.make_async_remote_copy(
                src_ref=outgoing.at[step - 1],
                dst_ref=arrived.at[step - 1],
                send_sem=z_send.at[step - 1],
                recv_sem=z_recv.at[step - 1],
                device_id={"ctx": block},
                device_id_type=MESH,
            )
            copy.start()
            z_copies.append(copy)
    for step in range(1, blocks):
        z_copies[step - 1].wait_recv()
        total += arrived[step - 1].astype(f32)
    grad_ref[...] = total
    weighed = stream_ref[...].astype(f32) * total * gain_ref[...]
    inner_own[...] = lax.dot_general(
        jnp.ones((8, width), f32),
        weighed,
        (((1,), (1,)), ((), ())),
        precision=lax.Precision.HIGHEST,
        preferred_element_type=f32,
    )
    i_copies = []
    for turn in range(1, parts):
        copy = pltpu.make_async_remote_copy(
            src_ref=inner_own,
            dst_ref=inner_all.at[turn - 1],
            send_sem=i_send.at[turn - 1],
            recv_sem=i_recv.at[turn - 1],
            device_id={"ep": lax.rem(my_ep + turn, parts)},
            device_id_type=MESH,
        )
        copy.start()
        i_copies.append(copy)
    inner = inner_own[...]
    for turn in range(1, parts):
        i_copies[turn - 1].wait_recv()
        inner += inner_all[turn - 1]
    inner_ref[...] = inner
    for copy in list(copies.values()) + z_copies + i_copies:
        copy.wait_send()


def combine(rows, picks, stream, gain, ident):
    blocks, capacity, _ = rows.shape
    parts = lax.axis_size("ep")
    tokens, width = stream.shape
    dma = pltpu.SemaphoreType.DMA
    vmem = pl.BlockSpec(memory_space=pltpu.VMEM)
    return pl.pallas_call(
        combine_kernel,
        out_shape=[
            jax.ShapeDtypeStruct((tokens, width), jnp.float32),
            jax.ShapeDtypeStruct((8, tokens), jnp.float32),
        ],
        in_specs=[pl.BlockSpec(memory_space=pl.ANY), vmem, vmem, vmem],
        out_specs=[vmem, vmem],
        scratch_shapes=[
            pltpu.VMEM((blocks, parts, capacity, width), jnp.bfloat16),
            pltpu.VMEM((blocks - 1, tokens, width), jnp.bfloat16),
            pltpu.VMEM((blocks - 1, tokens, width), jnp.bfloat16),
            pltpu.VMEM((8, tokens), jnp.float32),
            pltpu.VMEM((parts - 1, 8, tokens), jnp.float32),
            dma,
            dma((blocks, parts - 1)),
            dma((blocks, parts - 1)),
            dma((blocks - 1,)),
            dma((blocks - 1,)),
            dma((parts - 1,)),
            dma((parts - 1,)),
        ],
        compiler_params=pltpu.CompilerParams(
            collective_id=ident, has_side_effects=True, vmem_limit_bytes=24 * 1024 * 1024
        ),
        name=f"combine_{ident}",
    )(rows, picks, stream, gain)


def spread_kernel(block_ref, all_ref, z_send, z_recv, xy_send, xy_recv, pair_send, pair_recv, own_sem):
    rows, width = block_ref.shape
    blocks = lax.axis_size("ctx")
    chips = lax.axis_size("ep") // 2
    my_block = lax.axis_index("ctx")
    my_ep = lax.axis_index("ep")
    chip = my_ep // 2
    core = lax.rem(my_ep, 2)

    def at(block, place):
        row = pl.multiple_of(block * rows, rows)
        column = pl.multiple_of(place * width, width)
        return all_ref.at[pl.ds(row, rows), pl.ds(column, width)]

    barrier = pltpu.get_barrier_semaphore()
    for step in range(1, blocks):
        pl.semaphore_signal(
            barrier, inc=1, device_id={"ctx": lax.rem(my_block + step, blocks)}, device_id_type=MESH
        )
    for step in range(1, chips):
        pl.semaphore_signal(
            barrier,
            inc=1,
            device_id={"ep": 2 * lax.rem(chip + step, chips) + core},
            device_id_type=MESH,
        )
    pl.semaphore_signal(
        barrier, inc=1, device_id={"ep": 2 * chip + 1 - core}, device_id_type=MESH
    )
    pl.semaphore_wait(barrier, blocks + chips - 1)
    z_copies = []
    for step in range(1, blocks):
        copy = pltpu.make_async_remote_copy(
            src_ref=block_ref,
            dst_ref=at(my_block, my_ep),
            send_sem=z_send.at[step - 1],
            recv_sem=z_recv.at[step - 1],
            device_id={"ctx": lax.rem(my_block + step, blocks)},
            device_id_type=MESH,
        )
        copy.start()
        z_copies.append(copy)
    own = pltpu.make_async_copy(block_ref, at(my_block, my_ep), own_sem)
    own.start()
    xy_copies = {}
    pair_copies = []

    def to_pair(back, turn):
        block = lax.rem(my_block - back + blocks, blocks)
        place = 2 * lax.rem(chip - turn + chips, chips) + core
        source = block_ref if back == 0 and turn == 0 else at(block, place)
        copy = pltpu.make_async_remote_copy(
            src_ref=source,
            dst_ref=at(block, place),
            send_sem=pair_send.at[back * chips + turn],
            recv_sem=pair_recv.at[back * chips + turn],
            device_id={"ep": 2 * chip + 1 - core},
            device_id_type=MESH,
        )
        copy.start()
        pair_copies.append(copy)

    for back in range(blocks + 1):
        if back < blocks:
            block = lax.rem(my_block - back + blocks, blocks)
            if back > 0:
                z_copies[back - 1].wait_recv()
            for step in range(1, chips):
                slot = back * (chips - 1) + step - 1
                copy = pltpu.make_async_remote_copy(
                    src_ref=block_ref if back == 0 else at(block, my_ep),
                    dst_ref=at(block, my_ep),
                    send_sem=xy_send.at[slot],
                    recv_sem=xy_recv.at[slot],
                    device_id={"ep": 2 * lax.rem(chip + step, chips) + core},
                    device_id_type=MESH,
                )
                copy.start()
                xy_copies[back, step] = copy
            to_pair(back, 0)
        if back > 0:
            for step in range(1, chips):
                xy_copies[back - 1, step].wait_recv()
                to_pair(back - 1, step)
    own.wait()
    for copy in z_copies + list(xy_copies.values()):
        copy.wait_send()
    for copy in pair_copies:
        copy.wait()


def spread(block, ident):
    blocks = lax.axis_size("ctx")
    parts = lax.axis_size("ep")
    rows, width = block.shape
    if blocks * parts > 64 or width % 128:
        return lax.all_gather(
            lax.all_gather(block, "ep", axis=1, tiled=True), "ctx", axis=0, tiled=True
        )
    chips = parts // 2
    dma = pltpu.SemaphoreType.DMA
    return pl.pallas_call(
        spread_kernel,
        out_shape=jax.ShapeDtypeStruct((blocks * rows, parts * width), block.dtype),
        in_specs=[pl.BlockSpec(memory_space=pl.ANY)],
        out_specs=pl.BlockSpec(memory_space=pl.ANY),
        scratch_shapes=[
            dma((blocks - 1,)),
            dma((blocks - 1,)),
            dma((blocks * (chips - 1),)),
            dma((blocks * (chips - 1),)),
            dma((blocks * chips,)),
            dma((blocks * chips,)),
            dma,
        ],
        compiler_params=pltpu.CompilerParams(collective_id=ident, has_side_effects=True),
        name=f"spread_{ident}",
    )(block)

def head_normalize(attended, gain):
    factor = lax.rsqrt(jnp.mean(attended * attended, -1, keepdims=True) + 1e-06)
    return attended * factor * gain


def contract_last(left, right):
    return lax.dot_general(
        left, right, (((1,), (1,)), ((), ())), preferred_element_type=jnp.float32
    )


def local(
    query_act,
    key_act,
    value_act,
    state_init,
    head_gain,
    out_weight,
    stream_in,
    model_gain,
    expert_ids,
    expert_slots,
    route_gates,
    gate_weight,
    up_weight,
    down_weight,
    out_grad,
):
    f32 = jnp.float32
    bf16 = jnp.bfloat16
    high = lax.Precision.HIGHEST
    ep_count = lax.axis_size("ep")
    ctx_count = lax.axis_size("ctx")
    expert_count = ep_count // 2
    my_ep = lax.axis_index("ep")
    my_ctx = lax.axis_index("ctx")
    tokens_here = query_act.shape[0]
    head_count = state_init.shape[0]
    head_size = state_init.shape[1]
    heads_width = head_count * head_size
    model_width = model_gain.shape[0]
    columns = stream_in.shape[1]
    capacity = 5 * tokens_here // (2 * expert_count)
    slots_all = ctx_count * capacity
    w_cols = lax.all_gather(out_weight, "ctx", axis=0, tiled=True)
    query3 = query_act.reshape(tokens_here, head_count, head_size)
    key3 = key_act.reshape(tokens_here, head_count, head_size)
    value3 = value_act.reshape(tokens_here, head_count, head_size)
    kv_own = jnp.einsum("thd,the->hde", key3, value3, preferred_element_type=f32)
    meta = jnp.concatenate(
        [expert_ids.T.astype(f32), expert_slots.T.astype(f32), route_gates.T, route_gates.T], 0
    )
    grad_item = (
        (out_grad, whole_ref, (tokens_here, model_width), lanes(columns), "ep")
        if columns % 128 == 0
        else (out_grad, whole_ref, (ep_count, tokens_here, columns), leading, "ep")
    )
    kv_all, meta_all, grad_block = exchange(
        "ctx",
        1,
        [
            (kv_own.astype(bf16), whole_ref, (ctx_count,) + kv_own.shape, leading),
            (meta, whole_ref, (ctx_count,) + meta.shape, leading),
            grad_item,
        ],
    )
    if grad_block.ndim == 3:
        grad_block = jnp.moveaxis(grad_block, 0, 1).reshape(tokens_here, model_width)
    here_hits = (expert_ids[:, :, None] == lax.rem(my_ep, expert_count)) & (
        expert_slots[:, :, None] == jnp.arange(capacity)
    )
    here_select = jnp.sum(here_hits.astype(f32), 1).astype(bf16)
    here_gates = jnp.sum(jnp.where(here_hits, route_gates[:, :, None], 0.0), (0, 1))
    grad_own = lax.dot_general(
        here_select, grad_block, (((0,), (0,)), ((), ())), preferred_element_type=f32
    )
    grad_rows = lax.all_gather(
        (grad_own * here_gates[:, None]).astype(bf16), "ctx", axis=0, tiled=True
    )
    earlier = (jnp.arange(ctx_count) < my_ctx).astype(f32)
    prefix = state_init + jnp.sum(earlier[:, None, None, None] * kv_all.astype(f32), 0)
    causal = jnp.arange(tokens_here)[:, None] >= jnp.arange(tokens_here)[None, :]
    scores = jnp.einsum("thd,shd->hts", query3, key3, preferred_element_type=f32)
    scores_bf = jnp.where(causal[None], scores, 0.0).astype(bf16)
    inside = jnp.einsum("hts,she->the", scores_bf, value3, preferred_element_type=f32)
    from_state = jnp.einsum("thd,hde->the", query3.astype(f32), prefix, precision=high)
    attended = from_state + inside
    gain_heads = head_gain.reshape(head_count, head_size)
    normed_heads = (
        head_normalize(attended, gain_heads).astype(bf16).reshape(tokens_here, heads_width)
    )
    normed_all = exchange(
        "ep",
        2,
        [(normed_heads, whole_ref, (tokens_here, ep_count * heads_width), lanes(heads_width))],
    )[0]
    attn_proj = jnp.dot(normed_all, w_cols, preferred_element_type=f32)
    stream = (stream_in.astype(f32) + attn_proj).astype(bf16)
    stream_f = stream.astype(f32)
    gain_cols = lax.dynamic_slice_in_dim(model_gain, my_ep * columns, columns, 0)
    all_rows = spread(stream, 3).astype(f32)
    scale_all = lax.rsqrt(jnp.mean(all_rows * all_rows, -1, keepdims=True) + 1e-05)
    model_in = (all_rows * scale_all * model_gain).astype(bf16)
    row_scale = lax.dynamic_slice_in_dim(scale_all, my_ctx * tokens_here, tokens_here, 0)
    ids_all = meta_all[:, 0:2]
    slots_of = meta_all[:, 2:4]
    slot_iota = jnp.arange(capacity).astype(f32)
    my_expert = lax.rem(my_ep, expert_count).astype(f32)
    own_hits = (ids_all[:, :, None, :] == my_expert) & (
        slots_of[:, :, None, :] == slot_iota[None, None, :, None]
    )
    own_select = jnp.sum(own_hits.astype(f32), 1).astype(bf16)

    def pick_rows(rows):
        return jnp.einsum(
            "cst,ctd->csd",
            own_select,
            rows.reshape(ctx_count, tokens_here, model_width),
            preferred_element_type=f32,
        )

    w_gate = gate_weight[0]
    w_up = up_weight[0]
    w_down = down_weight[0]
    portion = pick_rows(model_in).astype(bf16).reshape(slots_all, model_width)
    pre_gate = contract_last(portion, w_gate)
    pre_up = contract_last(portion, w_up)
    gate_sig = jax.nn.sigmoid(pre_gate)
    activated = (pre_gate * gate_sig * pre_up).astype(bf16)
    half_out = lax.psum_scatter(
        jnp.dot(activated, w_down, preferred_element_type=f32).astype(bf16),
        "ctx",
        scatter_dimension=0,
        tiled=True,
    )
    grad_act = contract_last(grad_rows, w_down)
    grad_gate_pre = (grad_act * pre_up * gate_sig * (1.0 + pre_gate * (1.0 - gate_sig))).astype(
        bf16
    )
    grad_up_pre = (grad_act * pre_gate * gate_sig).astype(bf16)
    grad_half = (
        jnp.dot(grad_gate_pre, w_gate, preferred_element_type=f32)
        + jnp.dot(grad_up_pre, w_up, preferred_element_type=f32)
    ).astype(bf16)
    grad_half = grad_half.reshape(ctx_count, capacity, model_width)
    expert_of = jnp.arange(expert_count).astype(f32)
    hits = (ids_all[:, :, None, :, None] == expert_of[None, None, :, None, None]) & (
        slots_of[:, :, None, :, None] == slot_iota[None, None, None, None, :]
    )
    picks = jnp.sum(hits.astype(f32), 1).astype(bf16)
    if columns % 128 == 0 and ep_count * ctx_count <= 64:
        grad_model_in, inner_rows = combine(grad_half, picks, stream, gain_cols[None], 4)
        scaled_grad = grad_model_in * gain_cols
        inner_sum = inner_rows[0]
    else:
        grad_parts, part_of = column_parts(grad_half, ep_count)
        grad_back = exchange(
            "ep", 4, [(grad_parts, part_of, (ctx_count, ep_count, capacity, columns), second)]
        )[0].reshape(ctx_count, 2, expert_count, capacity, columns)
        grad_tokens = jnp.einsum(
            "cets,chesd->ctd", picks, grad_back, preferred_element_type=f32
        ).astype(bf16)
        grad_terms = exchange("ctx", 5, [(grad_tokens, leading, grad_tokens.shape, leading)])[0]
        grad_model_in = jnp.sum(grad_terms.astype(f32), 0)
        scaled_grad = grad_model_in * gain_cols
        inner_own = jnp.sum(stream_f * scaled_grad, -1)
        inner_terms = exchange(
            "ep",
            6,
            [
                (
                    jnp.broadcast_to(inner_own[None], (8, tokens_here)),
                    whole_ref,
                    (ep_count, 8, tokens_here),
                    leading,
                )
            ],
        )[0]
        inner_sum = jnp.sum(inner_terms[:, 0], 0)
    grad_out = out_grad.astype(f32)
    grad_stream = (
        grad_out
        + row_scale * scaled_grad
        - stream_f * row_scale**3 * inner_sum[:, None] / model_width
    ).astype(bf16)
    head_parts = contract_last(grad_stream, w_cols).astype(bf16)
    out_parts, out_of = column_parts(half_out, ep_count)
    head_terms, returned = exchange(
        "ep",
        7,
        [
            (head_parts, lanes(heads_width), (ep_count, tokens_here, heads_width), leading),
            (out_parts, out_of, (ep_count, capacity, columns), leading),
        ],
    )
    grad_heads = jnp.sum(head_terms.astype(f32), 0)
    local_hits = (expert_ids[:, :, None, None] == (jnp.arange(ep_count) % expert_count)[:, None]) & (
        expert_slots[:, :, None, None] == jnp.arange(capacity)
    )
    dest_weights = jnp.sum(
        local_hits.astype(f32) * route_gates[:, :, None, None], 1
    ).reshape(tokens_here, ep_count * capacity)
    expert_mix = jnp.dot(
        dest_weights, returned.reshape(ep_count * capacity, columns).astype(f32), precision=high
    )
    layer_out = (stream_f + expert_mix).astype(bf16)
    head_pull = jax.vjp(lambda value: head_normalize(value, gain_heads), attended)[1]
    grad_attended = head_pull(grad_heads.reshape(tokens_here, head_count, head_size))[0].astype(
        bf16
    )
    state_part = jnp.einsum("thd,the->hde", query3, grad_attended, preferred_element_type=f32)
    state_all = exchange(
        "ctx", 8, [(state_part.astype(bf16), whole_ref, (ctx_count,) + state_part.shape, leading)]
    )[0].astype(f32)
    after = (jnp.arange(ctx_count) > my_ctx).astype(f32)
    later_sum = jnp.sum(after[:, None, None, None] * state_all, 0)
    state_total = jnp.sum(state_all, 0)
    grad_scores = jnp.einsum("the,she->hts", grad_attended, value3, preferred_element_type=f32)
    grad_masked = jnp.where(causal[None], grad_scores, 0.0).astype(jnp.bfloat16)
    grad_att_f = grad_attended.astype(f32)
    grad_query = jnp.einsum("the,hde->thd", grad_att_f, prefix, precision=high) + jnp.einsum(
        "hts,shd->thd", grad_masked, key3, preferred_element_type=f32
    )
    grad_key = jnp.einsum(
        "the,hde->thd", value3.astype(f32), later_sum, precision=high
    ) + jnp.einsum("hts,thd->shd", grad_masked, query3, preferred_element_type=f32)
    grad_value = jnp.einsum(
        "thd,hde->the", key3.astype(f32), later_sum, precision=high
    ) + jnp.einsum("hts,the->she", scores_bf, grad_attended, preferred_element_type=f32)
    flat_shape = (tokens_here, head_count * head_size)
    return (
        layer_out,
        grad_query.astype(jnp.bfloat16).reshape(flat_shape),
        grad_key.astype(jnp.bfloat16).reshape(flat_shape),
        grad_value.astype(jnp.bfloat16).reshape(flat_shape),
        state_total,
        grad_stream,
    )


def solution(mesh):
    return jax.shard_map(
        local,
        mesh=mesh,
        in_specs=(
            P("ctx", "ep"),
            P("ctx", "ep"),
            P("ctx", "ep"),
            P("ep", None, None),
            P("ep"),
            P("ctx", "ep"),
            P("ctx", "ep"),
            P(),
            P("ctx", None),
            P("ctx", None),
            P("ctx", None),
            P("ep", "ctx", None),
            P("ep", "ctx", None),
            P("ep", "ctx", None),
            P("ctx", "ep"),
        ),
        out_specs=(
            P("ctx", "ep"),
            P("ctx", "ep"),
            P("ctx", "ep"),
            P("ctx", "ep"),
            P("ep", None, None),
            P("ctx", "ep"),
        ),
        check_vma=False,
    )
```

```python
import functools

import jax
import jax.numpy as jnp
from jax import lax
from jax.experimental import pallas as pl
from jax.experimental.pallas import tpu as pltpu
from jax.sharding import PartitionSpec as P

MESH = pl.DeviceIdType.MESH


def greet(axes):
    barrier = pltpu.get_barrier_semaphore()
    expected = 0
    for axis in axes:
        total = lax.axis_size(axis)
        for step in range(1, total):
            pl.semaphore_signal(
                barrier,
                inc=1,
                device_id={axis: lax.rem(lax.axis_index(axis) + step, total)},
                device_id_type=MESH,
            )
        expected += total - 1
    pl.semaphore_wait(barrier, expected)


def exchange_kernel(axes, sources, places, *refs):
    count = len(sources)
    inputs, outputs = refs[:count], refs[count : 2 * count]
    send_sem, recv_sem, own_sem = refs[2 * count :]
    greet(sorted(set(axes)))
    copies = []
    for item in range(count):
        axis = axes[item]
        total = lax.axis_size(axis)
        me = lax.axis_index(axis)
        for step in range(1, total):
            peer = lax.rem(me + step, total)
            copy = pltpu.make_async_remote_copy(
                src_ref=sources[item](inputs[item], peer),
                dst_ref=places[item](outputs[item], me),
                send_sem=send_sem.at[item, step - 1],
                recv_sem=recv_sem.at[item, step - 1],
                device_id={axis: peer},
                device_id_type=MESH,
            )
            copy.start()
            copies.append(copy)
    for item in range(count):
        me = lax.axis_index(axes[item])
        own = pltpu.make_async_copy(
            sources[item](inputs[item], me), places[item](outputs[item], me), own_sem.at[item]
        )
        own.start()
        copies.append(own)
    for copy in copies:
        copy.wait()


def whole_ref(ref, peer):
    return ref


def leading(ref, place):
    return ref.at[place]


def second(ref, place):
    return ref.at[:, place]


def lanes(width):
    def pick(ref, place):
        start = pl.multiple_of(place * width, width)
        if len(ref.shape) == 2:
            return ref.at[:, pl.ds(start, width)]
        return ref.at[:, :, pl.ds(start, width)]

    return pick


def exchange(axis, ident, items):
    axes = [item[4] if len(item) > 4 else axis for item in items]
    total = max(lax.axis_size(name) for name in axes)
    count = len(items)
    result = pl.pallas_call(
        functools.partial(
            exchange_kernel, axes, [item[1] for item in items], [item[3] for item in items]
        ),
        out_shape=[jax.ShapeDtypeStruct(item[2], item[0].dtype) for item in items],
        in_specs=[pl.BlockSpec(memory_space=pl.ANY)] * count,
        out_specs=[pl.BlockSpec(memory_space=pl.ANY)] * count,
        scratch_shapes=[
            pltpu.SemaphoreType.DMA((count, total - 1)),
            pltpu.SemaphoreType.DMA((count, total - 1)),
            pltpu.SemaphoreType.DMA((count,)),
        ],
        compiler_params=pltpu.CompilerParams(collective_id=ident, has_side_effects=True),
        name=f"exchange_{ident}",
    )(*[item[0] for item in items])
    return result


def column_parts(value, parts):
    width = value.shape[-1] // parts
    if width % 128 == 0:
        return value, lanes(width)
    split = value.reshape(value.shape[:-1] + (parts, width))
    return jnp.moveaxis(split, -2, 0), leading


def combine_kernel(
    rows_ref, picks_ref, stream_ref, gain_ref, grad_ref, inner_ref,
    landed, outgoing, arrived, inner_own, inner_all,
    own_sem, send_sem, recv_sem, z_send, z_recv, i_send, i_recv,
):
    f32 = jnp.float32
    blocks = lax.axis_size("ctx")
    parts = lax.axis_size("ep")
    experts = picks_ref.shape[1]
    width = stream_ref.shape[1]
    my_block = lax.axis_index("ctx")
    my_ep = lax.axis_index("ep")
    greet(["ctx", "ep"])

    def block_at(step):
        return lax.rem(my_block + step, blocks)

    def columns_of(place):
        return pl.ds(pl.multiple_of(place * width, width), width)

    order = list(range(1, blocks)) + [0]
    copies = {}
    for step in order:
        block = block_at(step)
        for turn in range(1, parts):
            peer = lax.rem(my_ep + turn, parts)
            copy = pltpu.make_async_remote_copy(
                src_ref=rows_ref.at[block, :, columns_of(peer)],
                dst_ref=landed.at[block, my_ep],
                send_sem=send_sem.at[step, turn - 1],
                recv_sem=recv_sem.at[step, turn - 1],
                device_id={"ep": peer},
                device_id_type=MESH,
            )
            copy.start()
            copies[step, turn] = copy
    own = pltpu.make_async_copy(
        rows_ref.at[:, :, columns_of(my_ep)], landed.at[:, my_ep], own_sem
    )
    own.start()
    own.wait()
    z_copies = []
    total = None
    for step in order:
        block = block_at(step)
        for turn in range(1, parts):
            copies[step, turn].wait_recv()
        total = jnp.dot(picks_ref[block, 0], landed[block, 0], preferred_element_type=f32)
        for place in range(1, parts):
            total += jnp.dot(
                picks_ref[block, place % experts],
                landed[block, place],
                preferred_element_type=f32,
            )
        if step:
            outgoing[step - 1] = total.astype(outgoing.dtype)
            copy = pltpu.make_async_remote_copy(
                src_ref=outgoing.at[step - 1],
                dst_ref=arrived.at[step - 1],
                send_sem=z_send.at[step - 1],
                recv_sem=z_recv.at[step - 1],
                device_id={"ctx": block},
                device_id_type=MESH,
            )
            copy.start()
            z_copies.append(copy)
    for step in range(1, blocks):
        z_copies[step - 1].wait_recv()
        total += arrived[step - 1].astype(f32)
    grad_ref[...] = total
    weighed = stream_ref[...].astype(f32) * total * gain_ref[...]
    inner_own[...] = lax.dot_general(
        jnp.ones((8, width), f32),
        weighed,
        (((1,), (1,)), ((), ())),
        precision=lax.Precision.HIGHEST,
        preferred_element_type=f32,
    )
    i_copies = []
    for turn in range(1, parts):
        copy = pltpu.make_async_remote_copy(
            src_ref=inner_own,
            dst_ref=inner_all.at[turn - 1],
            send_sem=i_send.at[turn - 1],
            recv_sem=i_recv.at[turn - 1],
            device_id={"ep": lax.rem(my_ep + turn, parts)},
            device_id_type=MESH,
        )
        copy.start()
        i_copies.append(copy)
    inner = inner_own[...]
    for turn in range(1, parts):
        i_copies[turn - 1].wait_recv()
        inner += inner_all[turn - 1]
    inner_ref[...] = inner
    for copy in list(copies.values()) + z_copies + i_copies:
        copy.wait_send()


def combine(rows, picks, stream, gain, ident):
    blocks, capacity, _ = rows.shape
    parts = lax.axis_size("ep")
    tokens, width = stream.shape
    dma = pltpu.SemaphoreType.DMA
    vmem = pl.BlockSpec(memory_space=pltpu.VMEM)
    return pl.pallas_call(
        combine_kernel,
        out_shape=[
            jax.ShapeDtypeStruct((tokens, width), jnp.float32),
            jax.ShapeDtypeStruct((8, tokens), jnp.float32),
        ],
        in_specs=[pl.BlockSpec(memory_space=pl.ANY), vmem, vmem, vmem],
        out_specs=[vmem, vmem],
        scratch_shapes=[
            pltpu.VMEM((blocks, parts, capacity, width), jnp.bfloat16),
            pltpu.VMEM((blocks - 1, tokens, width), jnp.bfloat16),
            pltpu.VMEM((blocks - 1, tokens, width), jnp.bfloat16),
            pltpu.VMEM((8, tokens), jnp.float32),
            pltpu.VMEM((parts - 1, 8, tokens), jnp.float32),
            dma,
            dma((blocks, parts - 1)),
            dma((blocks, parts - 1)),
            dma((blocks - 1,)),
            dma((blocks - 1,)),
            dma((parts - 1,)),
            dma((parts - 1,)),
        ],
        compiler_params=pltpu.CompilerParams(
            collective_id=ident, has_side_effects=True, vmem_limit_bytes=24 * 1024 * 1024
        ),
        name=f"combine_{ident}",
    )(rows, picks, stream, gain)


def dims(left, right):
    return (((left,), (right,)), ((), ()))


def dot32(left, right, contract):
    return lax.dot_general(left, right, contract, preferred_element_type=jnp.float32)


def dot_high(left, right, contract):
    return lax.dot_general(
        left.astype(jnp.float32),
        right,
        contract,
        precision=lax.Precision.HIGHEST,
        preferred_element_type=jnp.float32,
    )


def masked(scores):
    rows = lax.broadcasted_iota(jnp.int32, scores.shape, 0)
    cols = lax.broadcasted_iota(jnp.int32, scores.shape, 1)
    return jnp.where(rows >= cols, scores, 0.0).astype(jnp.bfloat16)


def head_slices(state_ref):
    heads, size = state_ref.shape[-3], state_ref.shape[-1]
    return [(head, slice(head * size, (head + 1) * size)) for head in range(heads)]


def attend_kernel(
    query_ref, key_ref, value_ref, init_ref, kv_ref, gain_ref, attended_ref, normed_ref, prefix_ref
):
    mine = lax.axis_index("ctx")
    for head, part in head_slices(init_ref):
        prefix = init_ref[head]
        for block in range(kv_ref.shape[0]):
            prefix += jnp.where(block < mine, kv_ref[block, head].astype(jnp.float32), 0.0)
        prefix_ref[head] = prefix
        query = query_ref[:, part]
        scores = masked(dot32(query, key_ref[:, part], dims(1, 1)))
        attended = dot_high(query, prefix, dims(1, 0)) + dot32(
            scores, value_ref[:, part], dims(1, 0)
        )
        attended_ref[:, part] = attended
        normed_ref[:, part] = head_normalize(attended, gain_ref[:, part]).astype(jnp.bfloat16)


def pull_kernel(terms_ref, attended_ref, gain_ref, query_ref, grad_ref, state_ref):
    for head, part in head_slices(state_ref):
        grad_heads = terms_ref[0, :, part].astype(jnp.float32)
        for place in range(1, terms_ref.shape[0]):
            grad_heads += terms_ref[place, :, part].astype(jnp.float32)
        attended = attended_ref[:, part]
        scaled = grad_heads * gain_ref[:, part]
        factor = lax.rsqrt(jnp.mean(attended * attended, -1, keepdims=True) + 1e-06)
        inner = jnp.mean(attended * scaled, -1, keepdims=True)
        grad = (factor * scaled - attended * (factor * factor * factor * inner)).astype(
            jnp.bfloat16
        )
        grad_ref[:, part] = grad
        state_ref[head] = dot32(query_ref[:, part], grad, dims(0, 0)).astype(jnp.bfloat16)


def finish_kernel(
    query_ref, key_ref, value_ref, grad_ref, prefix_ref, states_ref,
    grad_query_ref, grad_key_ref, grad_value_ref, total_ref,
):
    mine = lax.axis_index("ctx")
    for head, part in head_slices(prefix_ref):
        later = jnp.zeros(prefix_ref.shape[1:], jnp.float32)
        total = later
        for block in range(states_ref.shape[0]):
            state = states_ref[block, head].astype(jnp.float32)
            total += state
            later += jnp.where(block > mine, state, 0.0)
        total_ref[head] = total
        query, key, value, grad = (
            query_ref[:, part], key_ref[:, part], value_ref[:, part], grad_ref[:, part]
        )
        scores = masked(dot32(query, key, dims(1, 1)))
        grad_scores = masked(dot32(grad, value, dims(1, 1)))
        grad_query_ref[:, part] = (
            dot_high(grad, prefix_ref[head], dims(1, 1)) + dot32(grad_scores, key, dims(1, 0))
        ).astype(jnp.bfloat16)
        grad_key_ref[:, part] = (
            dot_high(value, later, dims(1, 1)) + dot32(grad_scores, query, dims(0, 0))
        ).astype(jnp.bfloat16)
        grad_value_ref[:, part] = (
            dot_high(key, later, dims(1, 0)) + dot32(scores, grad, dims(0, 0))
        ).astype(jnp.bfloat16)


def on_device(kernel, outputs, name, *operands):
    vmem = pl.BlockSpec(memory_space=pltpu.VMEM)
    return pl.pallas_call(
        kernel,
        out_shape=[jax.ShapeDtypeStruct(shape, kind) for shape, kind in outputs],
        in_specs=[vmem] * len(operands),
        out_specs=[vmem] * len(outputs),
        compiler_params=pltpu.CompilerParams(vmem_limit_bytes=24 * 1024 * 1024),
        name=name,
    )(*operands)


def spread_kernel(block_ref, all_ref, z_send, z_recv, xy_send, xy_recv, pair_send, pair_recv, own_sem):
    rows, width = block_ref.shape
    blocks = lax.axis_size("ctx")
    chips = lax.axis_size("ep") // 2
    my_block = lax.axis_index("ctx")
    my_ep = lax.axis_index("ep")
    chip = my_ep // 2
    core = lax.rem(my_ep, 2)

    def at(block, place):
        row = pl.multiple_of(block * rows, rows)
        column = pl.multiple_of(place * width, width)
        return all_ref.at[pl.ds(row, rows), pl.ds(column, width)]

    barrier = pltpu.get_barrier_semaphore()
    for step in range(1, blocks):
        pl.semaphore_signal(
            barrier, inc=1, device_id={"ctx": lax.rem(my_block + step, blocks)}, device_id_type=MESH
        )
    for step in range(1, chips):
        pl.semaphore_signal(
            barrier,
            inc=1,
            device_id={"ep": 2 * lax.rem(chip + step, chips) + core},
            device_id_type=MESH,
        )
    pl.semaphore_signal(
        barrier, inc=1, device_id={"ep": 2 * chip + 1 - core}, device_id_type=MESH
    )
    pl.semaphore_wait(barrier, blocks + chips - 1)
    z_copies = []
    for step in range(1, blocks):
        copy = pltpu.make_async_remote_copy(
            src_ref=block_ref,
            dst_ref=at(my_block, my_ep),
            send_sem=z_send.at[step - 1],
            recv_sem=z_recv.at[step - 1],
            device_id={"ctx": lax.rem(my_block + step, blocks)},
            device_id_type=MESH,
        )
        copy.start()
        z_copies.append(copy)
    own = pltpu.make_async_copy(block_ref, at(my_block, my_ep), own_sem)
    own.start()
    xy_copies = {}
    pair_copies = []

    def to_pair(back, turn):
        block = lax.rem(my_block - back + blocks, blocks)
        place = 2 * lax.rem(chip - turn + chips, chips) + core
        source = block_ref if back == 0 and turn == 0 else at(block, place)
        copy = pltpu.make_async_remote_copy(
            src_ref=source,
            dst_ref=at(block, place),
            send_sem=pair_send.at[back * chips + turn],
            recv_sem=pair_recv.at[back * chips + turn],
            device_id={"ep": 2 * chip + 1 - core},
            device_id_type=MESH,
        )
        copy.start()
        pair_copies.append(copy)

    for back in range(blocks + 1):
        if back < blocks:
            block = lax.rem(my_block - back + blocks, blocks)
            if back > 0:
                z_copies[back - 1].wait_recv()
            for step in range(1, chips):
                slot = back * (chips - 1) + step - 1
                copy = pltpu.make_async_remote_copy(
                    src_ref=block_ref if back == 0 else at(block, my_ep),
                    dst_ref=at(block, my_ep),
                    send_sem=xy_send.at[slot],
                    recv_sem=xy_recv.at[slot],
                    device_id={"ep": 2 * lax.rem(chip + step, chips) + core},
                    device_id_type=MESH,
                )
                copy.start()
                xy_copies[back, step] = copy
            to_pair(back, 0)
        if back > 0:
            for step in range(1, chips):
                xy_copies[back - 1, step].wait_recv()
                to_pair(back - 1, step)
    own.wait()
    for copy in z_copies + list(xy_copies.values()):
        copy.wait_send()
    for copy in pair_copies:
        copy.wait()


def spread(block, ident):
    blocks = lax.axis_size("ctx")
    parts = lax.axis_size("ep")
    rows, width = block.shape
    if blocks * parts > 64 or width % 128:
        return lax.all_gather(
            lax.all_gather(block, "ep", axis=1, tiled=True), "ctx", axis=0, tiled=True
        )
    chips = parts // 2
    dma = pltpu.SemaphoreType.DMA
    return pl.pallas_call(
        spread_kernel,
        out_shape=jax.ShapeDtypeStruct((blocks * rows, parts * width), block.dtype),
        in_specs=[pl.BlockSpec(memory_space=pl.ANY)],
        out_specs=pl.BlockSpec(memory_space=pl.ANY),
        scratch_shapes=[
            dma((blocks - 1,)),
            dma((blocks - 1,)),
            dma((blocks * (chips - 1),)),
            dma((blocks * (chips - 1),)),
            dma((blocks * chips,)),
            dma((blocks * chips,)),
            dma,
        ],
        compiler_params=pltpu.CompilerParams(collective_id=ident, has_side_effects=True),
        name=f"spread_{ident}",
    )(block)

def head_normalize(attended, gain):
    factor = lax.rsqrt(jnp.mean(attended * attended, -1, keepdims=True) + 1e-06)
    return attended * factor * gain


def contract_last(left, right):
    return lax.dot_general(
        left, right, (((1,), (1,)), ((), ())), preferred_element_type=jnp.float32
    )


def local(
    query_act,
    key_act,
    value_act,
    state_init,
    head_gain,
    out_weight,
    stream_in,
    model_gain,
    expert_ids,
    expert_slots,
    route_gates,
    gate_weight,
    up_weight,
    down_weight,
    out_grad,
):
    f32 = jnp.float32
    bf16 = jnp.bfloat16
    high = lax.Precision.HIGHEST
    ep_count = lax.axis_size("ep")
    ctx_count = lax.axis_size("ctx")
    expert_count = ep_count // 2
    my_ep = lax.axis_index("ep")
    my_ctx = lax.axis_index("ctx")
    tokens_here = query_act.shape[0]
    head_count = state_init.shape[0]
    head_size = state_init.shape[1]
    heads_width = head_count * head_size
    model_width = model_gain.shape[0]
    columns = stream_in.shape[1]
    capacity = 5 * tokens_here // (2 * expert_count)
    slots_all = ctx_count * capacity
    w_cols = lax.all_gather(out_weight, "ctx", axis=0, tiled=True)
    kv_own = jnp.stack(
        [
            dot32(
                key_act[:, head * head_size : (head + 1) * head_size],
                value_act[:, head * head_size : (head + 1) * head_size],
                dims(0, 0),
            )
            for head in range(head_count)
        ]
    )
    meta = jnp.concatenate(
        [expert_ids.T.astype(f32), expert_slots.T.astype(f32), route_gates.T, route_gates.T], 0
    )
    grad_item = (
        (out_grad, whole_ref, (tokens_here, model_width), lanes(columns), "ep")
        if columns % 128 == 0
        else (out_grad, whole_ref, (ep_count, tokens_here, columns), leading, "ep")
    )
    kv_all, meta_all, grad_block = exchange(
        "ctx",
        1,
        [
            (kv_own.astype(bf16), whole_ref, (ctx_count,) + kv_own.shape, leading),
            (meta, whole_ref, (ctx_count,) + meta.shape, leading),
            grad_item,
        ],
    )
    if grad_block.ndim == 3:
        grad_block = jnp.moveaxis(grad_block, 0, 1).reshape(tokens_here, model_width)
    here_hits = (expert_ids[:, :, None] == lax.rem(my_ep, expert_count)) & (
        expert_slots[:, :, None] == jnp.arange(capacity)
    )
    here_select = jnp.sum(here_hits.astype(f32), 1).astype(bf16)
    here_gates = jnp.sum(jnp.where(here_hits, route_gates[:, :, None], 0.0), (0, 1))
    grad_own = lax.dot_general(
        here_select, grad_block, (((0,), (0,)), ((), ())), preferred_element_type=f32
    )
    grad_rows = lax.all_gather(
        (grad_own * here_gates[:, None]).astype(bf16), "ctx", axis=0, tiled=True
    )
    flat_shape = (tokens_here, heads_width)
    gain_row = head_gain[None]
    attended, normed_heads, prefix = on_device(
        attend_kernel,
        [(flat_shape, f32), (flat_shape, bf16), (state_init.shape, f32)],
        "attend",
        query_act,
        key_act,
        value_act,
        state_init,
        kv_all,
        gain_row,
    )
    normed_all = exchange(
        "ep",
        2,
        [(normed_heads, whole_ref, (tokens_here, ep_count * heads_width), lanes(heads_width))],
    )[0]
    attn_proj = jnp.dot(normed_all, w_cols, preferred_element_type=f32)
    stream = (stream_in.astype(f32) + attn_proj).astype(bf16)
    stream_f = stream.astype(f32)
    gain_cols = lax.dynamic_slice_in_dim(model_gain, my_ep * columns, columns, 0)
    all_rows = spread(stream, 3).astype(f32)
    scale_all = lax.rsqrt(jnp.mean(all_rows * all_rows, -1, keepdims=True) + 1e-05)
    model_in = (all_rows * scale_all * model_gain).astype(bf16)
    row_scale = lax.dynamic_slice_in_dim(scale_all, my_ctx * tokens_here, tokens_here, 0)
    ids_all = meta_all[:, 0:2]
    slots_of = meta_all[:, 2:4]
    slot_iota = jnp.arange(capacity).astype(f32)
    my_expert = lax.rem(my_ep, expert_count).astype(f32)
    own_hits = (ids_all[:, :, None, :] == my_expert) & (
        slots_of[:, :, None, :] == slot_iota[None, None, :, None]
    )
    own_select = jnp.sum(own_hits.astype(f32), 1).astype(bf16)

    def pick_rows(rows):
        return jnp.einsum(
            "cst,ctd->csd",
            own_select,
            rows.reshape(ctx_count, tokens_here, model_width),
            preferred_element_type=f32,
        )

    w_gate = gate_weight[0]
    w_up = up_weight[0]
    w_down = down_weight[0]
    portion = pick_rows(model_in).astype(bf16).reshape(slots_all, model_width)
    pre_gate = contract_last(portion, w_gate)
    pre_up = contract_last(portion, w_up)
    gate_sig = jax.nn.sigmoid(pre_gate)
    activated = (pre_gate * gate_sig * pre_up).astype(bf16)
    half_out = lax.psum_scatter(
        jnp.dot(activated, w_down, preferred_element_type=f32).astype(bf16),
        "ctx",
        scatter_dimension=0,
        tiled=True,
    )
    grad_act = contract_last(grad_rows, w_down)
    grad_gate_pre = (grad_act * pre_up * gate_sig * (1.0 + pre_gate * (1.0 - gate_sig))).astype(
        bf16
    )
    grad_up_pre = (grad_act * pre_gate * gate_sig).astype(bf16)
    grad_half = (
        jnp.dot(grad_gate_pre, w_gate, preferred_element_type=f32)
        + jnp.dot(grad_up_pre, w_up, preferred_element_type=f32)
    ).astype(bf16)
    grad_half = grad_half.reshape(ctx_count, capacity, model_width)
    expert_of = jnp.arange(expert_count).astype(f32)
    hits = (ids_all[:, :, None, :, None] == expert_of[None, None, :, None, None]) & (
        slots_of[:, :, None, :, None] == slot_iota[None, None, None, None, :]
    )
    picks = jnp.sum(hits.astype(f32), 1).astype(bf16)
    if columns % 128 == 0 and ep_count * ctx_count <= 64:
        grad_model_in, inner_rows = combine(grad_half, picks, stream, gain_cols[None], 4)
        scaled_grad = grad_model_in * gain_cols
        inner_sum = inner_rows[0]
    else:
        grad_parts, part_of = column_parts(grad_half, ep_count)
        grad_back = exchange(
            "ep", 4, [(grad_parts, part_of, (ctx_count, ep_count, capacity, columns), second)]
        )[0].reshape(ctx_count, 2, expert_count, capacity, columns)
        grad_tokens = jnp.einsum(
            "cets,chesd->ctd", picks, grad_back, preferred_element_type=f32
        ).astype(bf16)
        grad_terms = exchange("ctx", 5, [(grad_tokens, leading, grad_tokens.shape, leading)])[0]
        grad_model_in = jnp.sum(grad_terms.astype(f32), 0)
        scaled_grad = grad_model_in * gain_cols
        inner_own = jnp.sum(stream_f * scaled_grad, -1)
        inner_terms = exchange(
            "ep",
            6,
            [
                (
                    jnp.broadcast_to(inner_own[None], (8, tokens_here)),
                    whole_ref,
                    (ep_count, 8, tokens_here),
                    leading,
                )
            ],
        )[0]
        inner_sum = jnp.sum(inner_terms[:, 0], 0)
    grad_out = out_grad.astype(f32)
    grad_stream = (
        grad_out
        + row_scale * scaled_grad
        - stream_f * row_scale**3 * inner_sum[:, None] / model_width
    ).astype(bf16)
    head_parts = contract_last(grad_stream, w_cols).astype(bf16)
    head_terms = exchange(
        "ep",
        7,
        [(head_parts, lanes(heads_width), (ep_count, tokens_here, heads_width), leading)],
    )[0]
    grad_attended, state_part = on_device(
        pull_kernel,
        [(flat_shape, bf16), (state_init.shape, bf16)],
        "pull",
        head_terms,
        attended,
        gain_row,
        query_act,
    )
    out_parts, out_of = column_parts(half_out, ep_count)
    state_all, returned = exchange(
        "ctx",
        8,
        [
            (state_part, whole_ref, (ctx_count,) + state_part.shape, leading),
            (out_parts, out_of, (ep_count, capacity, columns), leading, "ep"),
        ],
    )
    local_hits = (expert_ids[:, :, None, None] == (jnp.arange(ep_count) % expert_count)[:, None]) & (
        expert_slots[:, :, None, None] == jnp.arange(capacity)
    )
    dest_weights = jnp.sum(
        local_hits.astype(f32) * route_gates[:, :, None, None], 1
    ).reshape(tokens_here, ep_count * capacity)
    expert_mix = jnp.dot(
        dest_weights, returned.reshape(ep_count * capacity, columns).astype(f32), precision=high
    )
    layer_out = (stream_f + expert_mix).astype(bf16)
    grad_query, grad_key, grad_value, state_total = on_device(
        finish_kernel,
        [(flat_shape, bf16), (flat_shape, bf16), (flat_shape, bf16), (state_init.shape, f32)],
        "finish",
        query_act,
        key_act,
        value_act,
        grad_attended,
        prefix,
        state_all,
    )
    return layer_out, grad_query, grad_key, grad_value, state_total, grad_stream


def solution(mesh):
    return jax.shard_map(
        local,
        mesh=mesh,
        in_specs=(
            P("ctx", "ep"),
            P("ctx", "ep"),
            P("ctx", "ep"),
            P("ep", None, None),
            P("ep"),
            P("ctx", "ep"),
            P("ctx", "ep"),
            P(),
            P("ctx", None),
            P("ctx", None),
            P("ctx", None),
            P("ep", "ctx", None),
            P("ep", "ctx", None),
            P("ep", "ctx", None),
            P("ctx", "ep"),
        ),
        out_specs=(
            P("ctx", "ep"),
            P("ctx", "ep"),
            P("ctx", "ep"),
            P("ctx", "ep"),
            P("ep", None, None),
            P("ctx", "ep"),
        ),
        check_vma=False,
    )
```
